32 devices in a mesh: dp: 4 (over y, x), tensor: 8 (over z, core).
Axes of the slice: x: 2, y: 2, z: 4, core: 2. Of those that a mesh axis runs over, the one named last changes fastest.
Arguments:
- acts: bfloat16 [32, 512, 28672], P('dp', None, 'tensor'), may hold values from -6 to 6
- grads: bfloat16 [32, 512, 8192], P('dp', None, 'tensor'), may hold values from -6 to 6
- proj_in: bfloat16 [28672, 64], P('tensor'), may hold values from -0.03125 to 0.03125
- proj_out: bfloat16 [8192, 64], P('tensor'), may hold values from -0.0625 to 0.0625
- queries: float32 [256, 4096], P('dp', 'tensor'), may hold values from -6 to 6
Outputs:
- scores: float32 [32, 256], P('dp')
The draws below stay inside these ranges and needn't reach their ends.
All inputs are finite; a program needn't handle non-finite values.
Results may differ from the reference program's by a relative error of at most 0.0003.
Values sent between devices are 32-bit elements; how exact they have to be, the bound alone decides.
A program may use at most 128 MiB of HBM per device.

```python
import jax
import jax.numpy as jnp
from jax import lax

D = 8192
FF = 28672
RANK = 64
LENGTH = 512
EXAMPLES = 32
QUERIES = 256


def level_of(rng, shape, shards, smallest, high):
    level = 1.0
    for position, blocks in shards:
        steps = jax.random.uniform(jax.random.fold_in(jax.random.fold_in(rng, 6), position), (blocks,), jnp.float32, smallest / len(shards), high / len(shards))
        level = level * jnp.repeat(jnp.exp(steps), shape[position] // blocks).reshape((-1,) + (1,) * (len(shape) - 1 - position))
    return level


def noise(rng, shape, deviation, limit, pieces=(), kind=jnp.bfloat16):
    result = deviation * jax.random.normal(rng, shape, jnp.float32)
    if pieces:
        result = result * level_of(rng, shape, pieces, -0.22, 0.18)
    return jnp.clip(result, -limit, limit).astype(kind)


def setup_inputs(seed: int = 0) -> dict:
    keys = jax.random.split(jax.random.key(seed), 6)
    acts = noise(keys[0], (EXAMPLES, LENGTH, FF), 1.0, 6.0, ((0, 4), (2, 8)))
    grads = noise(keys[1], (EXAMPLES, LENGTH, D), 1.0, 6.0, ((0, 4), (2, 8)))
    proj_in = noise(keys[2], (FF, RANK), FF ** -0.5, 0.03125, ((0, 8),))
    proj_out = noise(keys[3], (D, RANK), D ** -0.5, 0.0625, ((0, 8),))
    queries = noise(keys[4], (QUERIES, RANK * RANK), 1.0, 6.0, ((0, 4), (1, 8)), jnp.float32)
    return dict(acts=acts, grads=grads, proj_in=proj_in, proj_out=proj_out, queries=queries)


def reference(acts, grads, proj_in, proj_out, queries):
    side_in = jnp.dot(acts.reshape(EXAMPLES * LENGTH, FF), proj_in, preferred_element_type=jnp.float32)
    side_out = jnp.dot(grads.reshape(EXAMPLES * LENGTH, D), proj_out, preferred_element_type=jnp.float32)
    side_in = side_in.reshape(EXAMPLES, LENGTH, RANK)
    side_out = side_out.reshape(EXAMPLES, LENGTH, RANK)
    encoding = jnp.einsum("eti,etj->eij", side_out, side_in, precision=lax.Precision.HIGHEST)
    encoding = (encoding * (LENGTH ** -0.5)).reshape(EXAMPLES, RANK * RANK)
    scores = jnp.einsum("ek,qk->eq", encoding, queries, precision=lax.Precision.HIGHEST)
    return scores / RANK
```

```python
import functools

import jax
import jax.numpy as jnp
from jax import lax
from jax.experimental import pallas as pl
from jax.experimental.pallas import tpu as pltpu
from jax.sharding import PartitionSpec as P

MESH = pl.DeviceIdType.MESH
CHUNK = 128
SLOTS = 4


def kernel(n_dp, n_tensor, acts, grads, proj_in, proj_out, queries, out,
           x, x_sem, w_in, w_out, w, w_sem,
           part, pair, pair_send, pair_recv, chain, chain_send, chain_recv,
           gram, enc, enc_send, enc_recv,
           q_all, q_own_sem, q_send, q_recv,
           score, score_send, score_recv):
    examples, length, width_in = acts.shape
    width = x.shape[2]
    rank = proj_in.shape[1]
    blocks = length // CHUNK
    each = examples // 4
    items = each * blocks
    line = n_tensor // 2

    me = lax.axis_index("tensor")
    me_dp = lax.axis_index("dp")
    place = me // 2
    core = me % 2
    sibling = me + 1 - 2 * core
    is_end = jnp.logical_or(place == 0, place == line - 1)
    near = jnp.where(place < line // 2, 1, 0)
    near_hops = jnp.where(near == 1, place, line - 1 - place)
    far_hops = line - 1 - near_hops

    def where_is(s, u):
        half = items // 2
        late = s // half
        direction = jnp.where(is_end, near + late - 2 * near * late, u)
        item = jnp.where(is_end, 2 * (s % half) + u, s)
        return direction, item

    def start_load(s):
        slot = s % SLOTS
        for u in range(2):
            direction, item = where_is(s, u)
            start = pl.multiple_of((item % blocks) * CHUNK, CHUNK)
            for owner in range(2):
                e = (direction * 2 + owner) * each + item // blocks
                rows = pl.ds((2 * u + owner) * CHUNK, CHUNK)
                pltpu.make_async_copy(
                    acts.at[e, pl.ds(start, CHUNK), :],
                    x.at[slot, rows, pl.ds(0, width_in)], x_sem.at[slot]).start()
                pltpu.make_async_copy(
                    grads.at[e, pl.ds(start, CHUNK), :],
                    x.at[slot, rows, pl.ds(width_in, width - width_in)], x_sem.at[slot]).start()

    barrier = pltpu.get_barrier_semaphore()
    for r in range(1, n_tensor):
        pl.semaphore_signal(barrier, inc=1, device_id={"tensor": (me + r) % n_tensor}, device_id_type=MESH)
    for r in range(1, n_dp):
        pl.semaphore_signal(barrier, inc=1, device_id={"dp": (me_dp + r) % n_dp}, device_id_type=MESH)

    load_in = pltpu.make_async_copy(proj_in, w_in, w_sem.at[0])
    load_out = pltpu.make_async_copy(proj_out, w_out, w_sem.at[1])
    load_in.start()
    load_out.start()
    for s in range(SLOTS - 1):
        start_load(s)
    q_own = pltpu.make_async_copy(queries, q_all.at[me_dp], q_own_sem)
    q_own.start()
    load_in.wait()
    load_out.wait()
    w[pl.ds(0, width_in), :] = jnp.concatenate([w_in[...], jnp.zeros_like(w_in)], axis=1)
    w[pl.ds(width_in, width - width_in), :] = jnp.concatenate([jnp.zeros_like(w_out), w_out[...]], axis=1)

    pl.semaphore_wait(barrier, n_tensor + n_dp - 2)

    def query_copy(r):
        return pltpu.make_async_remote_copy(
            src_ref=queries, dst_ref=q_all.at[me_dp], send_sem=q_send.at[r - 1], recv_sem=q_recv.at[r - 1],
            device_id={"dp": (me_dp + r) % n_dp}, device_id_type=MESH)

    for r in range(1, n_dp):
        query_copy(r).start()

    def pair_copy(direction, item):
        return pltpu.make_async_remote_copy(
            src_ref=part.at[direction, item, 1 - core], dst_ref=pair.at[direction, item],
            send_sem=pair_send.at[direction, item], recv_sem=pair_recv.at[direction, item],
            device_id={"tensor": sibling}, device_id_type=MESH)

    def chain_copy(direction, item):
        return pltpu.make_async_remote_copy(
            src_ref=part.at[direction, item, core], dst_ref=chain.at[direction, item],
            send_sem=chain_send.at[direction, item], recv_sem=chain_recv.at[direction, item],
            device_id={"tensor": (me + 4 * direction - 2 + n_tensor) % n_tensor}, device_id_type=MESH)

    group = enc.shape[1]

    def enc_rows(t):
        return pl.ds(pl.multiple_of((rank + t * rank // n_tensor) // group * group, group), group)

    def enc_copy(j, e, r):
        to = (me + r) % n_tensor
        return pltpu.make_async_remote_copy(
            src_ref=gram.at[j, enc_rows(to), :], dst_ref=enc.at[e],
            send_sem=enc_send.at[j, r - 1], recv_sem=enc_recv.at[e],
            device_id={"tensor": to}, device_id_type=MESH)

    def process(direction, item, hops):
        pair_copy(direction, item).wait_recv()
        part[direction, item, core] = part[direction, item, core] + pair[direction, item]

        @pl.when(hops > 0)
        def _():
            chain_copy(direction, item).wait_recv()
            part[direction, item, core] = part[direction, item, core] + chain[direction, item]

        @pl.when(hops < line - 1)
        def _():
            chain_copy(direction, item).start()

        @pl.when(hops == line - 1)
        def _():
            side = part[direction, item, core]
            j = item // blocks
            e = (direction * 2 + core) * each + j
            add = lax.dot_general(side, side, (((0,), (0,)), ((), ())),
                                  precision=lax.Precision.HIGHEST, preferred_element_type=jnp.float32)

            @pl.when(item % blocks == 0)
            def _():
                gram[j] = add

            @pl.when(item % blocks != 0)
            def _():
                gram[j] = gram[j] + add

            @pl.when(item % blocks == blocks - 1)
            def _():
                for r in range(1, n_tensor):
                    enc_copy(j, e, r).start()
                enc[e] = gram[j, enc_rows(me), :]

    def step(s, carry):
        @pl.when(s < items)
        def _():
            slot = s % SLOTS

            @pl.when(s + SLOTS - 1 < items)
            def _():
                start_load(s + SLOTS - 1)

            pltpu.make_async_copy(x.at[slot], x.at[slot], x_sem.at[slot]).wait()
            sides = jnp.dot(x[slot], w[...], preferred_element_type=jnp.float32)
            for u in range(2):
                direction, item = where_is(s, u)
                for owner in range(2):
                    part[direction, item, owner] = sides[(2 * u + owner) * CHUNK:(2 * u + owner + 1) * CHUNK]
                pair_copy(direction, item).start()

        first = jnp.where(is_end, 2 * (s - 1), s - 1 - 2 * near_hops)
        count = jnp.where(is_end, 2, 1)
        for u in range(2):
            item = first + u

            @pl.when(jnp.logical_and(u < count, jnp.logical_and(item >= 0, item < items)))
            def _():
                process(near, item, near_hops)

        item_far = s - 1 - 2 * far_hops

        @pl.when(jnp.logical_and(item_far >= 0, item_far < items))
        def _():
            process(1 - near, item_far, far_hops)

        return carry

    lax.fori_loop(0, items + 2 * (line - 1) + 1, step, 0)

    q_own.wait()
    for r in range(1, n_dp):
        query_copy(r).wait_recv()
    for e in range(examples):
        owner = (0 if e < examples // 2 else n_tensor - 2) + (e // each) % 2

        @pl.when(me != owner)
        def _():
            enc_copy(0, e, 1).wait_recv()

    per = rank // n_tensor
    lane = lax.broadcasted_iota(jnp.int32, (examples, 2 * rank), 1)
    shift = me * per % group // per
    total = None
    for m in range(per // 2):
        picked = None
        for v in range(group // per):
            low = enc[:, v * per + 2 * m, :]
            high = enc[:, v * per + 2 * m + 1, :]
            both = jnp.where(lane < rank, low, pltpu.roll(high, rank, 1))
            picked = both if picked is None else jnp.where(shift == v, both, picked)
        rows = q_all[:, :, pl.ds(2 * rank * m, 2 * rank)].reshape(-1, 2 * rank)
        add = lax.dot_general(picked, rows, (((1,), (1,)), ((), ())),
                              precision=lax.Precision.HIGHEST, preferred_element_type=jnp.float32)
        total = add if total is None else total + add
    score[me] = total

    def score_copy(r):
        return pltpu.make_async_remote_copy(
            src_ref=score.at[me], dst_ref=score.at[me],
            send_sem=score_send.at[r - 1], recv_sem=score_recv.at[r - 1],
            device_id={"tensor": (me + r) % n_tensor}, device_id_type=MESH)

    def score_arrival(r):
        frm = (me - r + n_tensor) % n_tensor
        return pltpu.make_async_remote_copy(
            src_ref=score.at[frm], dst_ref=score.at[frm],
            send_sem=score_send.at[r - 1], recv_sem=score_recv.at[r - 1],
            device_id={"tensor": (me + r) % n_tensor}, device_id_type=MESH)

    for r in range(1, n_tensor):
        score_copy(r).start()
    for r in range(1, n_tensor):
        score_arrival(r).wait_recv()
    result = score[0]
    for t in range(1, n_tensor):
        result = result + score[t]
    out[...] = result * (length ** (-0.5) / rank)

    for r in range(1, n_tensor):
        score_copy(r).wait_send()
    for r in range(1, n_dp):
        query_copy(r).wait_send()

    def drain(i, carry):
        for direction in range(2):
            pair_copy(direction, i).wait_send()
            hops = jnp.where(near == direction, near_hops, far_hops)

            @pl.when(hops < line - 1)
            def _():
                chain_copy(direction, i).wait_send()

        return carry

    lax.fori_loop(0, items, drain, 0)

    @pl.when(is_end)
    def _():
        for j in range(each):
            for r in range(1, n_tensor):
                enc_copy(j, 0, r).wait_send()


def per_device(acts, grads, proj_in, proj_out, queries):
    examples, length, width_in = acts.shape
    width_out = grads.shape[2]
    rank = proj_in.shape[1]
    n_dp, n_tensor = lax.axis_size("dp"), lax.axis_size("tensor")
    n_query = queries.shape[0] * n_dp
    items = examples // 4 * (length // CHUNK)
    width = width_in + width_out
    group = max(rank // n_tensor, 8)
    f32, bf16, dma = jnp.float32, jnp.bfloat16, pltpu.SemaphoreType.DMA
    anywhere = pl.BlockSpec(memory_space=pl.ANY)
    tokens = examples * length
    return pl.pallas_call(
        functools.partial(kernel, n_dp, n_tensor),
        out_shape=jax.ShapeDtypeStruct((examples, n_query), f32),
        in_specs=[anywhere] * 5,
        out_specs=pl.BlockSpec(memory_space=pltpu.VMEM),
        scratch_shapes=[
            pltpu.VMEM((SLOTS, 4 * CHUNK, width), bf16), dma((SLOTS,)),
            pltpu.VMEM((width_in, rank), bf16), pltpu.VMEM((width_out, rank), bf16),
            pltpu.VMEM((width, 2 * rank), bf16), dma((2,)),
            pltpu.VMEM((2, items, 2, CHUNK, 2 * rank), f32),
            pltpu.VMEM((2, items, CHUNK, 2 * rank), f32), dma((2, items)), dma((2, items)),
            pltpu.VMEM((2, items, CHUNK, 2 * rank), f32), dma((2, items)), dma((2, items)),
            pltpu.VMEM((examples // 4, 2 * rank, 2 * rank), f32),
            pltpu.VMEM((examples, group, 2 * rank), f32),
            dma((examples // 4, n_tensor - 1)), dma((examples,)),
            pltpu.VMEM((n_dp,) + queries.shape, f32), dma(()), dma((n_dp - 1,)), dma((n_dp - 1,)),
            pltpu.VMEM((n_tensor, examples, n_query), f32), dma((n_tensor - 1,)), dma((n_tensor - 1,)),
        ],
        compiler_params=pltpu.CompilerParams(
            collective_id=0, has_side_effects=True, vmem_limit_bytes=48 * 1024 * 1024),
        cost_estimate=pl.CostEstimate(
            flops=2 * tokens * width * rank, bytes_accessed=2 * tokens * width, transcendentals=0),
    )(acts, grads, proj_in, proj_out, queries)


def solution(mesh):
    in_specs = (
        P("dp", None, "tensor"),
        P("dp", None, "tensor"),
        P("tensor", None),
        P("tensor", None),
        P("dp", "tensor"),
    )
    out_specs = P("dp", None)
    return jax.shard_map(
        per_device, mesh=mesh, in_specs=in_specs, out_specs=out_specs, check_vma=False
    )
```

```python
import functools

import jax
import jax.numpy as jnp
from jax import lax
from jax.experimental import pallas as pl
from jax.experimental.pallas import tpu as pltpu
from jax.sharding import PartitionSpec as P

MESH = pl.DeviceIdType.MESH
CHUNK = 64
SLOTS = 5
BASE = 2
LAG = 3


def split(value):
    high = value.astype(jnp.bfloat16)
    return high, (value - high.astype(jnp.float32)).astype(jnp.bfloat16)


def dot(a, b, over):
    return lax.dot_general(a, b, ((over[:1], over[1:]), ((), ())), preferred_element_type=jnp.float32)


def kernel(n_dp, n_tensor, acts, grads, proj_in, proj_out, queries, out,
           x, x_sem, w_side, w, w_sem,
           part, pair, pair_send, pair_recv, chain, chain_send, chain_recv,
           gram, enc, enc_send, enc_recv,
           q_all, q_high, q_low, q_own_sem, q_send, q_recv,
           score, score_send, score_recv):
    examples, length, width_in = acts.shape
    width = x.shape[2]
    rank = proj_in.shape[0]
    blocks = length // CHUNK
    each = examples // 4
    items = each * blocks
    line = n_tensor // 2

    me = lax.axis_index("tensor")
    me_dp = lax.axis_index("dp")
    place = me // 2
    core = me % 2
    sibling = me + 1 - 2 * core
    is_end = jnp.logical_or(place == 0, place == line - 1)
    near = jnp.where(place < line // 2, 1, 0)
    near_hops = jnp.where(near == 1, place, line - 1 - place)
    far_hops = line - 1 - near_hops

    def where_is(s, u):
        half = items // 2
        late = s // half
        direction = jnp.where(is_end, near + late - 2 * near * late, u)
        item = jnp.where(is_end, 2 * (s % half) + u, s)
        return direction, item

    def start_load(s):
        slot = s % SLOTS
        for u in range(2):
            direction, item = where_is(s, u)
            start = pl.multiple_of((item % blocks) * CHUNK, CHUNK)
            for owner in range(2):
                e = (direction * 2 + owner) * each + item // blocks
                rows = pl.ds((2 * u + owner) * CHUNK, CHUNK)
                pltpu.make_async_copy(
                    acts.at[e, pl.ds(start, CHUNK), :],
                    x.at[slot, rows, pl.ds(0, width_in)], x_sem.at[slot]).start()
                pltpu.make_async_copy(
                    grads.at[e, pl.ds(start, CHUNK), :],
                    x.at[slot, rows, pl.ds(width_in, width - width_in)], x_sem.at[slot]).start()

    barrier = pltpu.get_barrier_semaphore()
    for r in range(1, n_tensor):
        pl.semaphore_signal(barrier, inc=1, device_id={"tensor": (me + r) % n_tensor}, device_id_type=MESH)
    for r in range(1, n_dp):
        pl.semaphore_signal(barrier, inc=1, device_id={"dp": (me_dp + r) % n_dp}, device_id_type=MESH)

    in_lanes, out_lanes = pl.ds(0, width_in), pl.ds(width_in, width - width_in)
    in_rows, out_rows = pl.ds(0, rank), pl.ds(rank, rank)
    load_in = pltpu.make_async_copy(proj_in, w_side.at[in_rows, in_lanes], w_sem.at[0])
    load_out = pltpu.make_async_copy(proj_out, w_side.at[out_rows, out_lanes], w_sem.at[1])
    load_in.start()
    load_out.start()
    for s in range(SLOTS - 1):
        start_load(s)
    q_own = pltpu.make_async_copy(queries, q_all.at[me_dp], q_own_sem)
    q_own.start()
    w_side[out_rows, in_lanes] = jnp.zeros((rank, width_in), w_side.dtype)
    w_side[in_rows, out_lanes] = jnp.zeros((rank, width - width_in), w_side.dtype)
    load_in.wait()
    load_out.wait()
    w[...] = w_side[...].T

    def query_copy(r):
        return pltpu.make_async_remote_copy(
            src_ref=queries, dst_ref=q_all.at[me_dp], send_sem=q_send.at[r - 1], recv_sem=q_recv.at[r - 1],
            device_id={"dp": (me_dp + r) % n_dp}, device_id_type=MESH)

    def pair_copy(direction, item):
        return pltpu.make_async_remote_copy(
            src_ref=part.at[direction, item, 1 - core], dst_ref=pair.at[direction, item],
            send_sem=pair_send.at[direction, item], recv_sem=pair_recv.at[direction, item],
            device_id={"tensor": sibling}, device_id_type=MESH)

    def chain_copy(direction, item):
        return pltpu.make_async_remote_copy(
            src_ref=part.at[direction, item, core], dst_ref=chain.at[direction, item],
            send_sem=chain_send.at[direction, item], recv_sem=chain_recv.at[direction, item],
            device_id={"tensor": (me + 4 * direction - 2 + n_tensor) % n_tensor}, device_id_type=MESH)

    group = enc.shape[1]

    def enc_rows(t):
        return pl.ds(pl.multiple_of((rank + t * rank // n_tensor) // group * group, group), group)

    def enc_copy(j, e, r):
        to = (me + r) % n_tensor
        return pltpu.make_async_remote_copy(
            src_ref=gram.at[j, enc_rows(to), :], dst_ref=enc.at[e],
            send_sem=enc_send.at[j, r - 1], recv_sem=enc_recv.at[e],
            device_id={"tensor": to}, device_id_type=MESH)

    def process(direction, item, hops):
        pair_copy(direction, item).wait_recv()
        part[direction, item, core] = part[direction, item, core] + pair[direction, item]

        @pl.when(hops > 0)
        def _():
            chain_copy(direction, item).wait_recv()
            part[direction, item, core] = part[direction, item, core] + chain[direction, item]

        @pl.when(hops < line - 1)
        def _():
            chain_copy(direction, item).start()

        @pl.when(hops == line - 1)
        def _():
            side = part[direction, item, core]
            j = item // blocks
            e = (direction * 2 + core) * each + j
            high, low = split(side)
            add = dot(jnp.concatenate([high, high, low], axis=0), jnp.concatenate([high, low, high], axis=0), (0, 0))

            @pl.when(item % blocks == 0)
            def _():
                gram[j] = add

            @pl.when(item % blocks != 0)
            def _():
                gram[j] = gram[j] + add

            @pl.when(item % blocks == blocks - 1)
            def _():
                for r in range(1, n_tensor):
                    enc_copy(j, e, r).start()
                enc[e] = gram[j, enc_rows(me), :]

    def step(s, carry):
        @pl.when(s < items)
        def _():
            slot = s % SLOTS

            @pl.when(s + SLOTS - 1 < items)
            def _():
                start_load(s + SLOTS - 1)

            pltpu.make_async_copy(x.at[slot], x.at[slot], x_sem.at[slot]).wait()
            sides = jnp.dot(x[slot], w[...], preferred_element_type=jnp.float32)
            for u in range(2):
                direction, item = where_is(s, u)
                for owner in range(2):
                    part[direction, item, owner] = sides[(2 * u + owner) * CHUNK:(2 * u + owner + 1) * CHUNK]

            @pl.when(s == 0)
            def _():
                pl.semaphore_wait(barrier, n_tensor + n_dp - 2)
                for r in range(1, n_dp):
                    query_copy(r).start()

            for u in range(2):
                direction, item = where_is(s, u)
                pair_copy(direction, item).start()

        @pl.when(s == items)
        def _():
            q_own.wait()
            for r in range(1, n_dp):
                query_copy(r).wait_recv()
            high, low = split(q_all[...].reshape(q_high.shape))
            q_high[...] = high
            q_low[...] = low

        first = jnp.where(is_end, 2 * (s - BASE), s - BASE - LAG * near_hops)
        count = jnp.where(is_end, 2, 1)
        for u in range(2):
            item = first + u

            @pl.when(jnp.logical_and(u < count, jnp.logical_and(item >= 0, item < items)))
            def _():
                process(near, item, near_hops)

        item_far = s - BASE - LAG * far_hops

        @pl.when(jnp.logical_and(item_far >= 0, item_far < items))
        def _():
            process(1 - near, item_far, far_hops)

        return carry

    lax.fori_loop(0, items + LAG * (line - 1) + BASE, step, 0)

    for e in range(examples):
        owner = (0 if e < examples // 2 else n_tensor - 2) + (e // each) % 2

        @pl.when(me != owner)
        def _():
            enc_copy(0, e, 1).wait_recv()

    per = rank // n_tensor
    lane = lax.broadcasted_iota(jnp.int32, (examples, 2 * rank), 1)
    shift = me * per % group // per
    columns = []
    for m in range(per // 2):
        picked = None
        for v in range(group // per):
            low = enc[:, v * per + 2 * m, :]
            high = enc[:, v * per + 2 * m + 1, :]
            both = jnp.where(lane < rank, low, pltpu.roll(high, rank, 1))
            picked = both if picked is None else jnp.where(shift == v, both, picked)
        columns.append(picked)
    high, low = split(jnp.concatenate(columns, axis=1))
    both = dot(jnp.concatenate([high, low], axis=0), q_high[...], (1, 1))
    score[me] = both[:examples] + both[examples:] + dot(high, q_low[...], (1, 1))

    def score_copy(r):
        return pltpu.make_async_remote_copy(
            src_ref=score.at[me], dst_ref=score.at[me],
            send_sem=score_send.at[r - 1], recv_sem=score_recv.at[r - 1],
            device_id={"tensor": (me + r) % n_tensor}, device_id_type=MESH)

    def score_arrival(r):
        frm = (me - r + n_tensor) % n_tensor
        return pltpu.make_async_remote_copy(
            src_ref=score.at[frm], dst_ref=score.at[frm],
            send_sem=score_send.at[r - 1], recv_sem=score_recv.at[r - 1],
            device_id={"tensor": (me + r) % n_tensor}, device_id_type=MESH)

    for r in range(1, n_tensor):
        score_copy(r).start()
    for r in range(1, n_tensor):
        score_arrival(r).wait_recv()
    result = score[0]
    for t in range(1, n_tensor):
        result = result + score[t]
    out[...] = result * (length ** (-0.5) / rank)

    for r in range(1, n_tensor):
        score_copy(r).wait_send()
    for r in range(1, n_dp):
        query_copy(r).wait_send()

    def drain(i, carry):
        for direction in range(2):
            pair_copy(direction, i).wait_send()
            hops = jnp.where(near == direction, near_hops, far_hops)

            @pl.when(hops < line - 1)
            def _():
                chain_copy(direction, i).wait_send()

        return carry

    lax.fori_loop(0, items, drain, 0)

    @pl.when(is_end)
    def _():
        for j in range(each):
            for r in range(1, n_tensor):
                enc_copy(j, 0, r).wait_send()


def per_device(acts, grads, proj_in, proj_out, queries):
    examples, length, width_in = acts.shape
    width_out = grads.shape[2]
    rank = proj_in.shape[1]
    n_dp, n_tensor = lax.axis_size("dp"), lax.axis_size("tensor")
    n_query = queries.shape[0] * n_dp
    items = examples // 4 * (length // CHUNK)
    width = width_in + width_out
    group = max(rank // n_tensor, 8)
    f32, bf16, dma = jnp.float32, jnp.bfloat16, pltpu.SemaphoreType.DMA
    in_hbm = pl.BlockSpec(memory_space=pltpu.HBM)
    tokens = examples * length
    return pl.pallas_call(
        functools.partial(kernel, n_dp, n_tensor),
        out_shape=jax.ShapeDtypeStruct((examples, n_query), f32),
        in_specs=[in_hbm] * 5,
        out_specs=pl.BlockSpec(memory_space=pltpu.VMEM),
        scratch_shapes=[
            pltpu.VMEM((SLOTS, 4 * CHUNK, width), bf16), dma((SLOTS,)),
            pltpu.VMEM((2 * rank, width), bf16), pltpu.VMEM((width, 2 * rank), bf16), dma((2,)),
            pltpu.VMEM((2, items, 2, CHUNK, 2 * rank), f32),
            pltpu.VMEM((2, items, CHUNK, 2 * rank), f32), dma((2, items)), dma((2, items)),
            pltpu.VMEM((2, items, CHUNK, 2 * rank), f32), dma((2, items)), dma((2, items)),
            pltpu.VMEM((examples // 4, 2 * rank, 2 * rank), f32),
            pltpu.VMEM((examples, group, 2 * rank), f32),
            dma((examples // 4, n_tensor - 1)), dma((examples,)),
            pltpu.VMEM((n_dp,) + queries.shape, f32),
            pltpu.VMEM((n_query, queries.shape[1]), bf16), pltpu.VMEM((n_query, queries.shape[1]), bf16), dma(()), dma((n_dp - 1,)), dma((n_dp - 1,)),
            pltpu.VMEM((n_tensor, examples, n_query), f32), dma((n_tensor - 1,)), dma((n_tensor - 1,)),
        ],
        compiler_params=pltpu.CompilerParams(
            collective_id=0, has_side_effects=True, vmem_limit_bytes=63 * 1024 * 1024),
        cost_estimate=pl.CostEstimate(
            flops=2 * tokens * width * rank, bytes_accessed=2 * tokens * width, transcendentals=0),
    )(acts, grads, proj_in.T, proj_out.T, queries)


def solution(mesh):
    in_specs = (
        P("dp", None, "tensor"),
        P("dp", None, "tensor"),
        P("tensor", None),
        P("tensor", None),
        P("dp", "tensor"),
    )
    out_specs = P("dp", None)
    return jax.shard_map(
        per_device, mesh=mesh, in_specs=in_specs, out_specs=out_specs, check_vma=False
    )
```

```python
import functools

import jax
import jax.numpy as jnp
from jax import lax
from jax.experimental import pallas as pl
from jax.experimental.pallas import tpu as pltpu
from jax.sharding import PartitionSpec as P

MESH = pl.DeviceIdType.MESH
CHUNK = 128
SLOTS = 4
BASE = 1
LAG = 2


def split(value):
    high = value.astype(jnp.bfloat16)
    return high, (value - high.astype(jnp.float32)).astype(jnp.bfloat16)


def dot(a, b, over):
    return lax.dot_general(a, b, ((over[:1], over[1:]), ((), ())), preferred_element_type=jnp.float32)


def kernel(n_dp, n_tensor, acts, grads, proj_in, proj_out, queries, out,
           x, x_sem, w_side, w, w_sem,
           part, pair, pair_send, pair_recv, chain, chain_send, chain_recv,
           gram, enc, enc_send, enc_recv,
           q_all, q_high, q_low, q_own_sem, q_send, q_recv,
           score, score_send, score_recv):
    examples, length, width_in = acts.shape
    width = x.shape[3]
    rank = proj_in.shape[0]
    blocks = length // CHUNK
    each = examples // 4
    items = each * blocks
    line = n_tensor // 2

    me = lax.axis_index("tensor")
    me_dp = lax.axis_index("dp")
    place = me // 2
    core = me % 2
    sibling = me + 1 - 2 * core
    is_end = jnp.logical_or(place == 0, place == line - 1)
    near = jnp.where(place < line // 2, 1, 0)
    near_hops = jnp.where(near == 1, place, line - 1 - place)
    far_hops = line - 1 - near_hops

    def where_is(s, u):
        half = items // 2
        late = s // half
        direction = jnp.where(is_end, near + late - 2 * near * late, u)
        item = jnp.where(is_end, 2 * (s % half) + u, s)
        return direction, item

    def start_load(s):
        slot = s % SLOTS
        for u in range(2):
            direction, item = where_is(s, u)
            start = pl.multiple_of((item % blocks) * CHUNK, CHUNK)
            e = direction * 2 * each + 2 * (item // blocks)
            pltpu.make_async_copy(
                acts.at[pl.ds(e, 2), pl.ds(start, CHUNK), :],
                x.at[slot, pl.ds(2 * u, 2), :, pl.ds(0, width_in)], x_sem.at[slot]).start()
            pltpu.make_async_copy(
                grads.at[pl.ds(e, 2), pl.ds(start, CHUNK), :],
                x.at[slot, pl.ds(2 * u, 2), :, pl.ds(width_in, width - width_in)], x_sem.at[slot]).start()

    barrier = pltpu.get_barrier_semaphore()
    for r in range(1, n_tensor):
        pl.semaphore_signal(barrier, inc=1, device_id={"tensor": (me + r) % n_tensor}, device_id_type=MESH)
    for r in range(1, n_dp):
        pl.semaphore_signal(barrier, inc=1, device_id={"dp": (me_dp + r) % n_dp}, device_id_type=MESH)

    in_lanes, out_lanes = pl.ds(0, width_in), pl.ds(width_in, width - width_in)
    in_rows, out_rows = pl.ds(0, rank), pl.ds(rank, rank)
    load_in = pltpu.make_async_copy(proj_in, w_side.at[in_rows, in_lanes], w_sem.at[0])
    load_out = pltpu.make_async_copy(proj_out, w_side.at[out_rows, out_lanes], w_sem.at[1])
    load_in.start()
    load_out.start()
    for s in range(SLOTS - 1):
        start_load(s)
    q_own = pltpu.make_async_copy(queries, q_all.at[me_dp], q_own_sem)
    q_own.start()
    w_side[out_rows, in_lanes] = jnp.zeros((rank, width_in), w_side.dtype)
    w_side[in_rows, out_lanes] = jnp.zeros((rank, width - width_in), w_side.dtype)
    load_in.wait()
    load_out.wait()
    w[...] = w_side[...].T

    def query_copy(r):
        return pltpu.make_async_remote_copy(
            src_ref=queries, dst_ref=q_all.at[me_dp], send_sem=q_send.at[r - 1], recv_sem=q_recv.at[r - 1],
            device_id={"dp": (me_dp + r) % n_dp}, device_id_type=MESH)

    def pair_copy(direction, item):
        return pltpu.make_async_remote_copy(
            src_ref=part.at[direction, item, 1 - core], dst_ref=pair.at[direction, item],
            send_sem=pair_send.at[direction, item], recv_sem=pair_recv.at[direction, item],
            device_id={"tensor": sibling}, device_id_type=MESH)

    def chain_copy(direction, item):
        return pltpu.make_async_remote_copy(
            src_ref=part.at[direction, item, core], dst_ref=chain.at[direction, item],
            send_sem=chain_send.at[direction, item], recv_sem=chain_recv.at[direction, item],
            device_id={"tensor": (me + 4 * direction - 2 + n_tensor) % n_tensor}, device_id_type=MESH)

    group = enc.shape[1]

    def enc_rows(t):
        return pl.ds(pl.multiple_of((rank + t * rank // n_tensor) // group * group, group), group)

    def enc_copy(j, e, r):
        to = (me + r) % n_tensor
        return pltpu.make_async_remote_copy(
            src_ref=gram.at[j, enc_rows(to), :], dst_ref=enc.at[e],
            send_sem=enc_send.at[j, r - 1], recv_sem=enc_recv.at[e],
            device_id={"tensor": to}, device_id_type=MESH)

    def process(direction, item, hops):
        pair_copy(direction, item).wait_recv()
        part[direction, item, core] = part[direction, item, core] + pair[direction, item]

        @pl.when(hops > 0)
        def _():
            chain_copy(direction, item).wait_recv()
            part[direction, item, core] = part[direction, item, core] + chain[direction, item]

        @pl.when(hops < line - 1)
        def _():
            chain_copy(direction, item).start()

        @pl.when(hops == line - 1)
        def _():
            side = part[direction, item, core]
            j = item // blocks
            e = direction * 2 * each + 2 * j + core
            high, low = split(side)
            add = dot(jnp.concatenate([high, high, low], axis=0), jnp.concatenate([high, low, high], axis=0), (0, 0))

            @pl.when(item % blocks == 0)
            def _():
                gram[j] = add

            @pl.when(item % blocks != 0)
            def _():
                gram[j] = gram[j] + add

            @pl.when(item % blocks == blocks - 1)
            def _():
                for r in range(1, n_tensor):
                    enc_copy(j, e, r).start()
                enc[e] = gram[j, enc_rows(me), :]

    def step(s, carry):
        @pl.when(s < items)
        def _():
            slot = s % SLOTS

            @pl.when(s + SLOTS - 1 < items)
            def _():
                start_load(s + SLOTS - 1)

            pltpu.make_async_copy(x.at[slot], x.at[slot], x_sem.at[slot]).wait()
            halves = []
            for h in range(2):
                lanes = pl.ds(h * (width // 2), width // 2)
                halves.append(dot(x[slot, :, :, lanes].reshape(4 * CHUNK, width // 2), w[lanes, :], (1, 0)))
            sides = halves[0] + halves[1]
            for u in range(2):
                direction, item = where_is(s, u)
                part[direction, item] = sides[2 * u * CHUNK:2 * (u + 1) * CHUNK].reshape(2, CHUNK, 2 * rank)

            @pl.when(s == 0)
            def _():
                pl.semaphore_wait(barrier, n_tensor + n_dp - 2)
                for r in range(1, n_dp):
                    query_copy(r).start()

            for u in range(2):
                direction, item = where_is(s, u)
                pair_copy(direction, item).start()

        @pl.when(s == items)
        def _():
            q_own.wait()
            for r in range(1, n_dp):
                query_copy(r).wait_recv()
            high, low = split(q_all[...].reshape(q_high.shape))
            q_high[...] = high
            q_low[...] = low

        first = jnp.where(is_end, 2 * (s - BASE), s - BASE - LAG * near_hops)
        count = jnp.where(is_end, 2, 1)
        for u in range(2):
            item = first + u

            @pl.when(jnp.logical_and(u < count, jnp.logical_and(item >= 0, item < items)))
            def _():
                process(near, item, near_hops)

        item_far = s - BASE - LAG * far_hops

        @pl.when(jnp.logical_and(item_far >= 0, item_far < items))
        def _():
            process(1 - near, item_far, far_hops)

        return carry

    lax.fori_loop(0, items + LAG * (line - 1) + BASE, step, 0)

    for e in range(examples):
        owner = (0 if e < examples // 2 else n_tensor - 2) + e % 2

        @pl.when(me != owner)
        def _():
            enc_copy(0, e, 1).wait_recv()

    per = rank // n_tensor
    lane = lax.broadcasted_iota(jnp.int32, (examples, 2 * rank), 1)
    shift = me * per % group // per
    columns = []
    for m in range(per // 2):
        picked = None
        for v in range(group // per):
            low = enc[:, v * per + 2 * m, :]
            high = enc[:, v * per + 2 * m + 1, :]
            both = jnp.where(lane < rank, low, pltpu.roll(high, rank, 1))
            picked = both if picked is None else jnp.where(shift == v, both, picked)
        columns.append(picked)
    high, low = split(jnp.concatenate(columns, axis=1))
    both = dot(jnp.concatenate([high, low], axis=0), q_high[...], (1, 1))
    score[me] = both[:examples] + both[examples:] + dot(high, q_low[...], (1, 1))

    def score_copy(r):
        return pltpu.make_async_remote_copy(
            src_ref=score.at[me], dst_ref=score.at[me],
            send_sem=score_send.at[r - 1], recv_sem=score_recv.at[r - 1],
            device_id={"tensor": (me + r) % n_tensor}, device_id_type=MESH)

    def score_arrival(r):
        frm = (me - r + n_tensor) % n_tensor
        return pltpu.make_async_remote_copy(
            src_ref=score.at[frm], dst_ref=score.at[frm],
            send_sem=score_send.at[r - 1], recv_sem=score_recv.at[r - 1],
            device_id={"tensor": (me + r) % n_tensor}, device_id_type=MESH)

    for r in range(1, n_tensor):
        score_copy(r).start()
    for r in range(1, n_tensor):
        score_arrival(r).wait_recv()
    result = score[0]
    for t in range(1, n_tensor):
        result = result + score[t]
    out[...] = result * (length ** (-0.5) / rank)

    for r in range(1, n_tensor):
        score_copy(r).wait_send()
    for r in range(1, n_dp):
        query_copy(r).wait_send()

    def drain(i, carry):
        for direction in range(2):
            pair_copy(direction, i).wait_send()
            hops = jnp.where(near == direction, near_hops, far_hops)

            @pl.when(hops < line - 1)
            def _():
                chain_copy(direction, i).wait_send()

        return carry

    lax.fori_loop(0, items, drain, 0)

    @pl.when(is_end)
    def _():
        for j in range(each):
            for r in range(1, n_tensor):
                enc_copy(j, 0, r).wait_send()


def per_device(acts, grads, proj_in, proj_out, queries):
    examples, length, width_in = acts.shape
    width_out = grads.shape[2]
    rank = proj_in.shape[1]
    n_dp, n_tensor = lax.axis_size("dp"), lax.axis_size("tensor")
    n_query = queries.shape[0] * n_dp
    items = examples // 4 * (length // CHUNK)
    width = width_in + width_out
    group = max(rank // n_tensor, 8)
    f32, bf16, dma = jnp.float32, jnp.bfloat16, pltpu.SemaphoreType.DMA
    in_hbm = pl.BlockSpec(memory_space=pltpu.HBM)
    tokens = examples * length
    return pl.pallas_call(
        functools.partial(kernel, n_dp, n_tensor),
        out_shape=jax.ShapeDtypeStruct((examples, n_query), f32),
        in_specs=[in_hbm] * 5,
        out_specs=pl.BlockSpec(memory_space=pltpu.VMEM),
        scratch_shapes=[
            pltpu.VMEM((SLOTS, 4, CHUNK, width), bf16), dma((SLOTS,)),
            pltpu.VMEM((2 * rank, width), bf16), pltpu.VMEM((width, 2 * rank), bf16), dma((2,)),
            pltpu.VMEM((2, items, 2, CHUNK, 2 * rank), f32),
            pltpu.VMEM((2, items, CHUNK, 2 * rank), f32), dma((2, items)), dma((2, items)),
            pltpu.VMEM((2, items, CHUNK, 2 * rank), f32), dma((2, items)), dma((2, items)),
            pltpu.VMEM((examples // 4, 2 * rank, 2 * rank), f32),
            pltpu.VMEM((examples, group, 2 * rank), f32),
            dma((examples // 4, n_tensor - 1)), dma((examples,)),
            pltpu.VMEM((n_dp,) + queries.shape, f32),
            pltpu.VMEM((n_query, queries.shape[1]), bf16), pltpu.VMEM((n_query, queries.shape[1]), bf16), dma(()), dma((n_dp - 1,)), dma((n_dp - 1,)),
            pltpu.VMEM((n_tensor, examples, n_query), f32), dma((n_tensor - 1,)), dma((n_tensor - 1,)),
        ],
        compiler_params=pltpu.CompilerParams(
            collective_id=0, has_side_effects=True, vmem_limit_bytes=63 * 1024 * 1024),
        cost_estimate=pl.CostEstimate(
            flops=2 * tokens * width * rank, bytes_accessed=2 * tokens * width, transcendentals=0),
    )(acts, grads, proj_in.T, proj_out.T, queries)


def solution(mesh):
    in_specs = (
        P("dp", None, "tensor"),
        P("dp", None, "tensor"),
        P("tensor", None),
        P("tensor", None),
        P("dp", "tensor"),
    )
    out_specs = P("dp", None)
    return jax.shard_map(
        per_device, mesh=mesh, in_specs=in_specs, out_specs=out_specs, check_vma=False
    )
```

```python
import functools

import jax
import jax.numpy as jnp
from jax import lax
from jax.experimental import pallas as pl
from jax.experimental.pallas import tpu as pltpu
from jax.sharding import PartitionSpec as P

MESH = pl.DeviceIdType.MESH
CHUNK = 128
SLOTS = 3
BASE = 1
EXTRA = 2


def split(value):
    high = value.astype(jnp.bfloat16)
    return high, (value - high.astype(jnp.float32)).astype(jnp.bfloat16)


def dot(a, b, over):
    return lax.dot_general(a, b, ((over[:1], over[1:]), ((), ())), preferred_element_type=jnp.float32)


def kernel(n_dp, n_tensor, acts, grads, proj_in, proj_out, queries, out,
           x, x_sem, w_side, w, w_sem,
           part, pair, pair_send, pair_recv, chain, chain_send, chain_recv,
           gram, enc, enc_send, enc_recv,
           q_all, q_high, q_low, q_own_sem, q_send, q_recv,
           score, score_send, score_recv):
    examples, length, width_in = acts.shape
    width = x.shape[3]
    rank = proj_in.shape[0]
    blocks = length // CHUNK
    each = examples // 4
    items = each * blocks
    line = n_tensor // 2

    me = lax.axis_index("tensor")
    me_dp = lax.axis_index("dp")
    place = me // 2
    core = me % 2
    sibling = me + 1 - 2 * core
    is_end = jnp.logical_or(place == 0, place == line - 1)
    near = jnp.where(place < line // 2, 1, 0)
    near_hops = jnp.where(near == 1, place, line - 1 - place)
    far_hops = line - 1 - near_hops

    def where_is(s, u):
        half = items // 2
        late = s // half
        direction = jnp.where(is_end, near + late - 2 * near * late, u)
        item = jnp.where(is_end, 2 * (s % half) + u, s)
        return direction, item

    def start_load(s):
        slot = s % SLOTS
        for u in range(2):
            direction, item = where_is(s, u)
            start = pl.multiple_of((item % blocks) * CHUNK, CHUNK)
            e = direction * 2 * each + 2 * (item // blocks)
            pltpu.make_async_copy(
                acts.at[pl.ds(e, 2), pl.ds(start, CHUNK), :],
                x.at[slot, pl.ds(2 * u, 2), :, pl.ds(0, width_in)], x_sem.at[slot]).start(priority=1)
            pltpu.make_async_copy(
                grads.at[pl.ds(e, 2), pl.ds(start, CHUNK), :],
                x.at[slot, pl.ds(2 * u, 2), :, pl.ds(width_in, width - width_in)], x_sem.at[slot]).start(priority=1)

    barrier = pltpu.get_barrier_semaphore()
    for r in range(1, n_tensor):
        pl.semaphore_signal(barrier, inc=1, device_id={"tensor": (me + r) % n_tensor}, device_id_type=MESH)
    for r in range(1, n_dp):
        pl.semaphore_signal(barrier, inc=1, device_id={"dp": (me_dp + r) % n_dp}, device_id_type=MESH)

    in_lanes, out_lanes = pl.ds(0, width_in), pl.ds(width_in, width - width_in)
    in_rows, out_rows = pl.ds(0, rank), pl.ds(rank, rank)
    load_in = pltpu.make_async_copy(proj_in, w_side.at[in_rows, in_lanes], w_sem.at[0])
    load_out = pltpu.make_async_copy(proj_out, w_side.at[out_rows, out_lanes], w_sem.at[1])
    load_in.start()
    load_out.start()
    for s in range(SLOTS - 1):
        start_load(s)
    q_own = pltpu.make_async_copy(queries, q_all.at[me_dp], q_own_sem)
    q_own.start()
    w_side[out_rows, in_lanes] = jnp.zeros((rank, width_in), w_side.dtype)
    w_side[in_rows, out_lanes] = jnp.zeros((rank, width - width_in), w_side.dtype)
    load_in.wait()
    load_out.wait()
    w[...] = w_side[...].T

    def query_copy(r):
        return pltpu.make_async_remote_copy(
            src_ref=queries, dst_ref=q_all.at[me_dp], send_sem=q_send.at[r - 1], recv_sem=q_recv.at[r - 1],
            device_id={"dp": (me_dp + r) % n_dp}, device_id_type=MESH)

    def pair_copy(direction, item):
        return pltpu.make_async_remote_copy(
            src_ref=part.at[direction, item, 1 - core], dst_ref=pair.at[direction, item],
            send_sem=pair_send.at[direction, item], recv_sem=pair_recv.at[direction, item],
            device_id={"tensor": sibling}, device_id_type=MESH)

    def chain_copy(direction, item):
        return pltpu.make_async_remote_copy(
            src_ref=part.at[direction, item, core], dst_ref=chain.at[direction, item],
            send_sem=chain_send.at[direction, item], recv_sem=chain_recv.at[direction, item],
            device_id={"tensor": (me + 4 * direction - 2 + n_tensor) % n_tensor}, device_id_type=MESH)

    group = enc.shape[1]

    def enc_rows(t):
        return pl.ds(pl.multiple_of((rank + t * rank // n_tensor) // group * group, group), group)

    def enc_copy(j, e, r):
        to = (me + r) % n_tensor
        return pltpu.make_async_remote_copy(
            src_ref=gram.at[j, enc_rows(to), :], dst_ref=enc.at[e],
            send_sem=enc_send.at[j, r - 1], recv_sem=enc_recv.at[e],
            device_id={"tensor": to}, device_id_type=MESH)

    def lag(hops):
        return BASE + hops + jnp.where(hops >= line // 2, EXTRA, 0)

    def process(direction, item, hops):
        pair_copy(direction, item).wait_recv()
        part[direction, item, core] = part[direction, item, core] + pair[direction, item]

        @pl.when(hops > 0)
        def _():
            chain_copy(direction, item).wait_recv()
            part[direction, item, core] = part[direction, item, core] + chain[direction, item]

        @pl.when(hops < line - 1)
        def _():
            chain_copy(direction, item).start()

        @pl.when(hops == line - 1)
        def _():
            side = part[direction, item, core]
            j = item // blocks
            e = direction * 2 * each + 2 * j + core
            high, low = split(side)
            add = dot(jnp.concatenate([high, high, low], axis=0), jnp.concatenate([high, low, high], axis=0), (0, 0))

            @pl.when(item % blocks == 0)
            def _():
                gram[j] = add

            @pl.when(item % blocks != 0)
            def _():
                gram[j] = gram[j] + add

            @pl.when(item % blocks == blocks - 1)
            def _():
                for r in range(1, n_tensor):
                    enc_copy(j, e, r).start()
                enc[e] = gram[j, enc_rows(me), :]

    def step(s, carry):
        @pl.when(s < items)
        def _():
            slot = s % SLOTS

            @pl.when(s + SLOTS - 1 < items)
            def _():
                start_load(s + SLOTS - 1)

            pltpu.make_async_copy(x.at[slot], x.at[slot], x_sem.at[slot]).wait()
            halves = []
            for h in range(2):
                lanes = pl.ds(h * (width // 2), width // 2)
                halves.append(dot(x[slot, :, :, lanes].reshape(4 * CHUNK, width // 2), w[lanes, :], (1, 0)))
            sides = halves[0] + halves[1]
            for u in range(2):
                direction, item = where_is(s, u)
                part[direction, item] = sides[2 * u * CHUNK:2 * (u + 1) * CHUNK].reshape(2, CHUNK, 2 * rank)

            @pl.when(s == 0)
            def _():
                pl.semaphore_wait(barrier, n_tensor + n_dp - 2)
                for r in range(1, n_dp):
                    query_copy(r).start()

            for u in range(2):
                direction, item = where_is(s, u)
                pair_copy(direction, item).start()

        @pl.when(s == items)
        def _():
            q_own.wait()
            for r in range(1, n_dp):
                query_copy(r).wait_recv()
            high, low = split(q_all[...].reshape(q_high.shape))
            q_high[...] = high
            q_low[...] = low

        first = jnp.where(is_end, 2 * (s - BASE), s - lag(near_hops))
        count = jnp.where(is_end, 2, 1)
        for u in range(2):
            item = first + u

            @pl.when(jnp.logical_and(u < count, jnp.logical_and(item >= 0, item < items)))
            def _():
                process(near, item, near_hops)

        item_far = s - lag(far_hops)

        @pl.when(jnp.logical_and(item_far >= 0, item_far < items))
        def _():
            process(1 - near, item_far, far_hops)

        return carry

    lax.fori_loop(0, items + BASE + line - 1 + EXTRA, step, 0)

    for e in range(examples):
        owner = (0 if e < examples // 2 else n_tensor - 2) + e % 2

        @pl.when(me != owner)
        def _():
            enc_copy(0, e, 1).wait_recv()

    per = rank // n_tensor
    lane = lax.broadcasted_iota(jnp.int32, (examples, 2 * rank), 1)
    shift = me * per % group // per
    columns = []
    for m in range(per // 2):
        picked = None
        for v in range(group // per):
            low = enc[:, v * per + 2 * m, :]
            high = enc[:, v * per + 2 * m + 1, :]
            both = jnp.where(lane < rank, low, pltpu.roll(high, rank, 1))
            picked = both if picked is None else jnp.where(shift == v, both, picked)
        columns.append(picked)
    high, low = split(jnp.concatenate(columns, axis=1))
    both = dot(jnp.concatenate([high, low], axis=0), q_high[...], (1, 1))
    score[me] = both[:examples] + both[examples:] + dot(high, q_low[...], (1, 1))

    def score_copy(r):
        return pltpu.make_async_remote_copy(
            src_ref=score.at[me], dst_ref=score.at[me],
            send_sem=score_send.at[r - 1], recv_sem=score_recv.at[r - 1],
            device_id={"tensor": (me + r) % n_tensor}, device_id_type=MESH)

    def score_arrival(r):
        frm = (me - r + n_tensor) % n_tensor
        return pltpu.make_async_remote_copy(
            src_ref=score.at[frm], dst_ref=score.at[frm],
            send_sem=score_send.at[r - 1], recv_sem=score_recv.at[r - 1],
            device_id={"tensor": (me + r) % n_tensor}, device_id_type=MESH)

    for r in range(1, n_tensor):
        score_copy(r).start()
    for r in range(1, n_tensor):
        score_arrival(r).wait_recv()
    result = score[0]
    for t in range(1, n_tensor):
        result = result + score[t]
    out[...] = result * (length ** (-0.5) / rank)

    for r in range(1, n_tensor):
        score_copy(r).wait_send()
    for r in range(1, n_dp):
        query_copy(r).wait_send()

    def drain(i, carry):
        for direction in range(2):
            pair_copy(direction, i).wait_send()
            hops = jnp.where(near == direction, near_hops, far_hops)

            @pl.when(hops < line - 1)
            def _():
                chain_copy(direction, i).wait_send()

        return carry

    lax.fori_loop(0, items, drain, 0)

    @pl.when(is_end)
    def _():
        for j in range(each):
            for r in range(1, n_tensor):
                enc_copy(j, 0, r).wait_send()


def per_device(acts, grads, proj_in, proj_out, queries):
    examples, length, width_in = acts.shape
    width_out = grads.shape[2]
    rank = proj_in.shape[1]
    n_dp, n_tensor = lax.axis_size("dp"), lax.axis_size("tensor")
    n_query = queries.shape[0] * n_dp
    items = examples // 4 * (length // CHUNK)
    width = width_in + width_out
    group = max(rank // n_tensor, 8)
    f32, bf16, dma = jnp.float32, jnp.bfloat16, pltpu.SemaphoreType.DMA
    in_hbm = pl.BlockSpec(memory_space=pltpu.HBM)
    tokens = examples * length
    return pl.pallas_call(
        functools.partial(kernel, n_dp, n_tensor),
        out_shape=jax.ShapeDtypeStruct((examples, n_query), f32),
        in_specs=[in_hbm] * 5,
        out_specs=pl.BlockSpec(memory_space=pltpu.VMEM),
        scratch_shapes=[
            pltpu.VMEM((SLOTS, 4, CHUNK, width), bf16), dma((SLOTS,)),
            pltpu.VMEM((2 * rank, width), bf16), pltpu.VMEM((width, 2 * rank), bf16), dma((2,)),
            pltpu.VMEM((2, items, 2, CHUNK, 2 * rank), f32),
            pltpu.VMEM((2, items, CHUNK, 2 * rank), f32), dma((2, items)), dma((2, items)),
            pltpu.VMEM((2, items, CHUNK, 2 * rank), f32), dma((2, items)), dma((2, items)),
            pltpu.VMEM((examples // 4, 2 * rank, 2 * rank), f32),
            pltpu.VMEM((examples, group, 2 * rank), f32),
            dma((examples // 4, n_tensor - 1)), dma((examples,)),
            pltpu.VMEM((n_dp,) + queries.shape, f32),
            pltpu.VMEM((n_query, queries.shape[1]), bf16), pltpu.VMEM((n_query, queries.shape[1]), bf16), dma(()), dma((n_dp - 1,)), dma((n_dp - 1,)),
            pltpu.VMEM((n_tensor, examples, n_query), f32), dma((n_tensor - 1,)), dma((n_tensor - 1,)),
        ],
        compiler_params=pltpu.CompilerParams(
            collective_id=0, has_side_effects=True, vmem_limit_bytes=63 * 1024 * 1024),
        cost_estimate=pl.CostEstimate(
            flops=2 * tokens * width * rank, bytes_accessed=2 * tokens * width, transcendentals=0),
    )(acts, grads, proj_in.T, proj_out.T, queries)


def solution(mesh):
    in_specs = (
        P("dp", None, "tensor"),
        P("dp", None, "tensor"),
        P("tensor", None),
        P("tensor", None),
        P("dp", "tensor"),
    )
    out_specs = P("dp", None)
    return jax.shard_map(
        per_device, mesh=mesh, in_specs=in_specs, out_specs=out_specs, check_vma=False
    )
```

```python
import functools

import jax
import jax.numpy as jnp
from jax import lax
from jax.experimental import pallas as pl
from jax.experimental.pallas import tpu as pltpu
from jax.sharding import PartitionSpec as P

MESH = pl.DeviceIdType.MESH
CHUNK = 128
SLOTS = 3
BASE = 1
EXTRA = 2


def split(value):
    high = value.astype(jnp.bfloat16)
    return high, (value - high.astype(jnp.float32)).astype(jnp.bfloat16)


def dot(a, b, over):
    return lax.dot_general(a, b, ((over[:1], over[1:]), ((), ())), preferred_element_type=jnp.float32)


def kernel(n_dp, n_tensor, acts, grads, proj_in, proj_out, queries, out,
           x, x_sem, w_in, w_out, w_sem,
           part, pair, pair_send, pair_recv, chain, chain_send, chain_recv,
           gram, enc, enc_send, enc_recv,
           q_all, q_high, q_low, q_own_sem, q_send, q_recv,
           score, score_send, score_recv):
    examples, length, width_in = acts.shape
    width = x.shape[3]
    rank = proj_in.shape[0]
    blocks = length // CHUNK
    each = examples // 4
    items = each * blocks
    line = n_tensor // 2

    me = lax.axis_index("tensor")
    me_dp = lax.axis_index("dp")
    place = me // 2
    core = me % 2
    sibling = me + 1 - 2 * core
    is_end = jnp.logical_or(place == 0, place == line - 1)
    near = jnp.where(place < line // 2, 1, 0)
    near_hops = jnp.where(near == 1, place, line - 1 - place)
    far_hops = line - 1 - near_hops

    def where_is(s, u):
        half = items // 2
        late = s // half
        direction = jnp.where(is_end, near + late - 2 * near * late, u)
        item = jnp.where(is_end, 2 * (s % half) + u, s)
        return direction, item

    def start_load(s):
        slot = s % SLOTS
        for u in range(2):
            direction, item = where_is(s, u)
            start = pl.multiple_of((item % blocks) * CHUNK, CHUNK)
            e = direction * 2 * each + 2 * (item // blocks)
            pltpu.make_async_copy(
                acts.at[pl.ds(e, 2), pl.ds(start, CHUNK), :],
                x.at[slot, pl.ds(2 * u, 2), :, pl.ds(0, width_in)], x_sem.at[slot]).start(priority=1)
            pltpu.make_async_copy(
                grads.at[pl.ds(e, 2), pl.ds(start, CHUNK), :],
                x.at[slot, pl.ds(2 * u, 2), :, pl.ds(width_in, width - width_in)], x_sem.at[slot]).start(priority=1)

    barrier = pltpu.get_barrier_semaphore()
    for r in range(1, n_tensor):
        pl.semaphore_signal(barrier, inc=1, device_id={"tensor": (me + r) % n_tensor}, device_id_type=MESH)
    for r in range(1, n_dp):
        pl.semaphore_signal(barrier, inc=1, device_id={"dp": (me_dp + r) % n_dp}, device_id_type=MESH)

    load_in = pltpu.make_async_copy(proj_in, w_in, w_sem.at[0])
    load_out = pltpu.make_async_copy(proj_out, w_out, w_sem.at[1])
    load_in.start()
    load_out.start()
    for s in range(SLOTS - 1):
        start_load(s)
    q_own = pltpu.make_async_copy(queries, q_all.at[me_dp], q_own_sem)
    q_own.start()
    load_in.wait()
    load_out.wait()

    def query_copy(r):
        return pltpu.make_async_remote_copy(
            src_ref=queries, dst_ref=q_all.at[me_dp], send_sem=q_send.at[r - 1], recv_sem=q_recv.at[r - 1],
            device_id={"dp": (me_dp + r) % n_dp}, device_id_type=MESH)

    def pair_copy(direction, item):
        return pltpu.make_async_remote_copy(
            src_ref=part.at[direction, item, 1 - core], dst_ref=pair.at[direction, item],
            send_sem=pair_send.at[direction, item], recv_sem=pair_recv.at[direction, item],
            device_id={"tensor": sibling}, device_id_type=MESH)

    def chain_copy(direction, item):
        return pltpu.make_async_remote_copy(
            src_ref=part.at[direction, item, core], dst_ref=chain.at[direction, item],
            send_sem=chain_send.at[direction, item], recv_sem=chain_recv.at[direction, item],
            device_id={"tensor": (me + 4 * direction - 2 + n_tensor) % n_tensor}, device_id_type=MESH)

    group = enc.shape[1]

    def enc_rows(t):
        return pl.ds(pl.multiple_of((rank + t * rank // n_tensor) // group * group, group), group)

    def enc_copy(j, e, r):
        to = (me + r) % n_tensor
        return pltpu.make_async_remote_copy(
            src_ref=gram.at[j, enc_rows(to), :], dst_ref=enc.at[e],
            send_sem=enc_send.at[j, r - 1], recv_sem=enc_recv.at[e],
            device_id={"tensor": to}, device_id_type=MESH)

    def lag(hops):
        return BASE + hops + jnp.where(hops >= line // 2, EXTRA, 0)

    def process(direction, item, hops):
        pair_copy(direction, item).wait_recv()
        part[direction, item, core] = part[direction, item, core] + pair[direction, item]

        @pl.when(hops > 0)
        def _():
            chain_copy(direction, item).wait_recv()
            part[direction, item, core] = part[direction, item, core] + chain[direction, item]

        @pl.when(hops < line - 1)
        def _():
            chain_copy(direction, item).start()

        @pl.when(hops == line - 1)
        def _():
            side = part[direction, item, core]
            j = item // blocks
            e = direction * 2 * each + 2 * j + core
            high, low = split(side)
            add = dot(jnp.concatenate([high, high, low], axis=1), jnp.concatenate([high, low, high], axis=1), (1, 1))

            @pl.when(item % blocks == 0)
            def _():
                gram[j] = add

            @pl.when(item % blocks != 0)
            def _():
                gram[j] = gram[j] + add

            @pl.when(item % blocks == blocks - 1)
            def _():
                for r in range(1, n_tensor):
                    enc_copy(j, e, r).start()
                enc[e] = gram[j, enc_rows(me), :]

    def step(s, carry):
        @pl.when(s < items)
        def _():
            slot = s % SLOTS

            @pl.when(s + SLOTS - 1 < items)
            def _():
                start_load(s + SLOTS - 1)

            pltpu.make_async_copy(x.at[slot], x.at[slot], x_sem.at[slot]).wait()
            tokens_in = x[slot, :, :, pl.ds(0, width_in)].reshape(4 * CHUNK, width_in)
            tokens_out = x[slot, :, :, pl.ds(width_in, width - width_in)].reshape(4 * CHUNK, width - width_in)
            sides_in = dot(w_in[...], tokens_in, (1, 1))
            sides_out = dot(w_out[...], tokens_out, (1, 1))
            for u in range(2):
                direction, item = where_is(s, u)
                for owner in range(2):
                    lanes = slice((2 * u + owner) * CHUNK, (2 * u + owner + 1) * CHUNK)
                    part[direction, item, owner, pl.ds(0, rank), :] = sides_in[:, lanes]
                    part[direction, item, owner, pl.ds(rank, rank), :] = sides_out[:, lanes]

            @pl.when(s == 0)
            def _():
                pl.semaphore_wait(barrier, n_tensor + n_dp - 2)
                for r in range(1, n_dp):
                    query_copy(r).start()

            for u in range(2):
                direction, item = where_is(s, u)
                pair_copy(direction, item).start()

        @pl.when(s == items)
        def _():
            q_own.wait()
            for r in range(1, n_dp):
                query_copy(r).wait_recv()
            high, low = split(q_all[...].reshape(q_high.shape))
            q_high[...] = high
            q_low[...] = low

        first = jnp.where(is_end, 2 * (s - BASE), s - lag(near_hops))
        count = jnp.where(is_end, 2, 1)
        for u in range(2):
            item = first + u

            @pl.when(jnp.logical_and(u < count, jnp.logical_and(item >= 0, item < items)))
            def _():
                process(near, item, near_hops)

        item_far = s - lag(far_hops)

        @pl.when(jnp.logical_and(item_far >= 0, item_far < items))
        def _():
            process(1 - near, item_far, far_hops)

        return carry

    lax.fori_loop(0, items + BASE + line - 1 + EXTRA, step, 0)

    for e in range(examples):
        owner = (0 if e < examples // 2 else n_tensor - 2) + e % 2

        @pl.when(me != owner)
        def _():
            enc_copy(0, e, 1).wait_recv()

    per = rank // n_tensor
    lane = lax.broadcasted_iota(jnp.int32, (examples, 2 * rank), 1)
    shift = me * per % group // per
    columns = []
    for m in range(per // 2):
        picked = None
        for v in range(group // per):
            low = enc[:, v * per + 2 * m, :]
            high = enc[:, v * per + 2 * m + 1, :]
            both = jnp.where(lane < rank, low, pltpu.roll(high, rank, 1))
            picked = both if picked is None else jnp.where(shift == v, both, picked)
        columns.append(picked)
    high, low = split(jnp.concatenate(columns, axis=1))
    both = dot(jnp.concatenate([high, low], axis=0), q_high[...], (1, 1))
    score[me] = both[:examples] + both[examples:] + dot(high, q_low[...], (1, 1))

    def score_copy(r):
        return pltpu.make_async_remote_copy(
            src_ref=score.at[me], dst_ref=score.at[me],
            send_sem=score_send.at[r - 1], recv_sem=score_recv.at[r - 1],
            device_id={"tensor": (me + r) % n_tensor}, device_id_type=MESH)

    def score_arrival(r):
        frm = (me - r + n_tensor) % n_tensor
        return pltpu.make_async_remote_copy(
            src_ref=score.at[frm], dst_ref=score.at[frm],
            send_sem=score_send.at[r - 1], recv_sem=score_recv.at[r - 1],
            device_id={"tensor": (me + r) % n_tensor}, device_id_type=MESH)

    for r in range(1, n_tensor):
        score_copy(r).start()
    for r in range(1, n_tensor):
        score_arrival(r).wait_recv()
    result = score[0]
    for t in range(1, n_tensor):
        result = result + score[t]
    out[...] = result * (length ** (-0.5) / rank)

    for r in range(1, n_tensor):
        score_copy(r).wait_send()
    for r in range(1, n_dp):
        query_copy(r).wait_send()

    def drain(i, carry):
        for direction in range(2):
            pair_copy(direction, i).wait_send()
            hops = jnp.where(near == direction, near_hops, far_hops)

            @pl.when(hops < line - 1)
            def _():
                chain_copy(direction, i).wait_send()

        return carry

    lax.fori_loop(0, items, drain, 0)

    @pl.when(is_end)
    def _():
        for j in range(each):
            for r in range(1, n_tensor):
                enc_copy(j, 0, r).wait_send()


def per_device(acts, grads, proj_in, proj_out, queries):
    examples, length, width_in = acts.shape
    width_out = grads.shape[2]
    rank = proj_in.shape[1]
    n_dp, n_tensor = lax.axis_size("dp"), lax.axis_size("tensor")
    n_query = queries.shape[0] * n_dp
    items = examples // 4 * (length // CHUNK)
    width = width_in + width_out
    group = max(rank // n_tensor, 8)
    f32, bf16, dma = jnp.float32, jnp.bfloat16, pltpu.SemaphoreType.DMA
    in_hbm = pl.BlockSpec(memory_space=pltpu.HBM)
    tokens = examples * length
    return pl.pallas_call(
        functools.partial(kernel, n_dp, n_tensor),
        out_shape=jax.ShapeDtypeStruct((examples, n_query), f32),
        in_specs=[in_hbm] * 5,
        out_specs=pl.BlockSpec(memory_space=pltpu.VMEM),
        scratch_shapes=[
            pltpu.VMEM((SLOTS, 4, CHUNK, width), bf16), dma((SLOTS,)),
            pltpu.VMEM((rank, width_in), bf16), pltpu.VMEM((rank, width_out), bf16), dma((2,)),
            pltpu.VMEM((2, items, 2, 2 * rank, CHUNK), f32),
            pltpu.VMEM((2, items, 2 * rank, CHUNK), f32), dma((2, items)), dma((2, items)),
            pltpu.VMEM((2, items, 2 * rank, CHUNK), f32), dma((2, items)), dma((2, items)),
            pltpu.VMEM((examples // 4, 2 * rank, 2 * rank), f32),
            pltpu.VMEM((examples, group, 2 * rank), f32),
            dma((examples // 4, n_tensor - 1)), dma((examples,)),
            pltpu.VMEM((n_dp,) + queries.shape, f32),
            pltpu.VMEM((n_query, queries.shape[1]), bf16), pltpu.VMEM((n_query, queries.shape[1]), bf16), dma(()), dma((n_dp - 1,)), dma((n_dp - 1,)),
            pltpu.VMEM((n_tensor, examples, n_query), f32), dma((n_tensor - 1,)), dma((n_tensor - 1,)),
        ],
        compiler_params=pltpu.CompilerParams(
            collective_id=0, has_side_effects=True, vmem_limit_bytes=63 * 1024 * 1024),
        cost_estimate=pl.CostEstimate(
            flops=2 * tokens * width * rank, bytes_accessed=2 * tokens * width, transcendentals=0),
    )(acts, grads, proj_in.T, proj_out.T, queries)


def solution(mesh):
    in_specs = (
        P("dp", None, "tensor"),
        P("dp", None, "tensor"),
        P("tensor", None),
        P("tensor", None),
        P("dp", "tensor"),
    )
    out_specs = P("dp", None)
    return jax.shard_map(
        per_device, mesh=mesh, in_specs=in_specs, out_specs=out_specs, check_vma=False
    )
```

```python
import functools

import jax
import jax.numpy as jnp
from jax import lax
from jax.experimental import pallas as pl
from jax.experimental.pallas import tpu as pltpu
from jax.sharding import PartitionSpec as P

MESH = pl.DeviceIdType.MESH
CHUNK = 128
SLOTS = 3
BASE = 1
EXTRA = 1


def split(value):
    high = value.astype(jnp.bfloat16)
    return high, (value - high.astype(jnp.float32)).astype(jnp.bfloat16)


def dot(a, b, over):
    return lax.dot_general(a, b, ((over[:1], over[1:]), ((), ())), preferred_element_type=jnp.float32)


def kernel(n_dp, n_tensor, acts, grads, proj_in, proj_out, queries, out,
           x, x_sem, w_side, w, w_sem,
           part, pair, pair_send, pair_recv, chain, chain_send, chain_recv,
           gram, enc, enc_send, enc_recv,
           q_all, q_high, q_low, q_own_sem, q_send, q_recv,
           score, score_send, score_recv):
    examples, length, width_in = acts.shape
    width = x.shape[3]
    rank = proj_in.shape[0]
    blocks = length // CHUNK
    each = examples // 4
    items = each * blocks
    line = n_tensor // 2

    me = lax.axis_index("tensor")
    me_dp = lax.axis_index("dp")
    place = me // 2
    core = me % 2
    sibling = me + 1 - 2 * core
    is_end = jnp.logical_or(place == 0, place == line - 1)
    near = jnp.where(place < line // 2, 1, 0)
    near_hops = jnp.where(near == 1, place, line - 1 - place)
    far_hops = line - 1 - near_hops

    def where_is(s, u):
        half = items // 2
        late = s // half
        first, last = s == 0, s == items - 1
        if u == 0:
            between = jnp.where(last, 1 - near, near)
            item = jnp.where(first, 0, jnp.where(last, items - 2, s + 1))
        else:
            between = jnp.where(first, near, 1 - near)
            item = jnp.where(first, 1, jnp.where(last, items - 1, s - 1))
        direction = jnp.where(is_end, near + late - 2 * near * late, between)
        item = jnp.where(is_end, 2 * (s % half) + u, item)
        return direction, item

    def start_load(s):
        slot = s % SLOTS
        for u in range(2):
            direction, item = where_is(s, u)
            start = pl.multiple_of((item % blocks) * CHUNK, CHUNK)
            e = direction * 2 * each + 2 * (item // blocks)
            pltpu.make_async_copy(
                acts.at[pl.ds(e, 2), pl.ds(start, CHUNK), :],
                x.at[slot, pl.ds(2 * u, 2), :, pl.ds(0, width_in)], x_sem.at[slot]).start(priority=1)
            pltpu.make_async_copy(
                grads.at[pl.ds(e, 2), pl.ds(start, CHUNK), :],
                x.at[slot, pl.ds(2 * u, 2), :, pl.ds(width_in, width - width_in)], x_sem.at[slot]).start(priority=1)

    barrier = pltpu.get_barrier_semaphore()
    for r in range(1, n_tensor):
        pl.semaphore_signal(barrier, inc=1, device_id={"tensor": (me + r) % n_tensor}, device_id_type=MESH)
    for r in range(1, n_dp):
        pl.semaphore_signal(barrier, inc=1, device_id={"dp": (me_dp + r) % n_dp}, device_id_type=MESH)

    in_lanes, out_lanes = pl.ds(0, width_in), pl.ds(width_in, width - width_in)
    in_rows, out_rows = pl.ds(0, rank), pl.ds(rank, rank)
    load_in = pltpu.make_async_copy(proj_in, w_side.at[in_rows, in_lanes], w_sem.at[0])
    load_out = pltpu.make_async_copy(proj_out, w_side.at[out_rows, out_lanes], w_sem.at[1])
    load_in.start()
    load_out.start()
    for s in range(SLOTS - 1):
        start_load(s)
    q_own = pltpu.make_async_copy(queries, q_all.at[me_dp], q_own_sem)
    q_own.start()
    w_side[out_rows, in_lanes] = jnp.zeros((rank, width_in), w_side.dtype)
    w_side[in_rows, out_lanes] = jnp.zeros((rank, width - width_in), w_side.dtype)
    load_in.wait()
    load_out.wait()
    w[...] = w_side[...].T

    def query_copy(r):
        return pltpu.make_async_remote_copy(
            src_ref=queries, dst_ref=q_all.at[me_dp], send_sem=q_send.at[r - 1], recv_sem=q_recv.at[r - 1],
            device_id={"dp": (me_dp + r) % n_dp}, device_id_type=MESH)

    def pair_copy(direction, item):
        return pltpu.make_async_remote_copy(
            src_ref=part.at[direction, item, 1 - core], dst_ref=pair.at[direction, item],
            send_sem=pair_send.at[direction, item], recv_sem=pair_recv.at[direction, item],
            device_id={"tensor": sibling}, device_id_type=MESH)

    def chain_copy(direction, item):
        return pltpu.make_async_remote_copy(
            src_ref=part.at[direction, item, core], dst_ref=chain.at[direction, item],
            send_sem=chain_send.at[direction, item], recv_sem=chain_recv.at[direction, item],
            device_id={"tensor": (me + 4 * direction - 2 + n_tensor) % n_tensor}, device_id_type=MESH)

    group = enc.shape[1]

    def enc_rows(t):
        return pl.ds(pl.multiple_of((rank + t * rank // n_tensor) // group * group, group), group)

    def enc_copy(j, e, r):
        to = (me + jnp.where(place < line // 2, r, n_tensor - r)) % n_tensor
        return pltpu.make_async_remote_copy(
            src_ref=gram.at[j, enc_rows(to), :], dst_ref=enc.at[e],
            send_sem=enc_send.at[j, r - 1], recv_sem=enc_recv.at[e],
            device_id={"tensor": to}, device_id_type=MESH)

    far_lag = jnp.where(is_end, max(line - 1 + EXTRA, items // 2 + BASE), far_hops + EXTRA)

    def process(direction, item, hops):
        pair_copy(direction, item).wait_recv()
        part[direction, item, core] = part[direction, item, core] + pair[direction, item]

        @pl.when(hops > 0)
        def _():
            chain_copy(direction, item).wait_recv()
            part[direction, item, core] = part[direction, item, core] + chain[direction, item]

        @pl.when(hops < line - 1)
        def _():
            chain_copy(direction, item).start()

        @pl.when(hops == line - 1)
        def _():
            side = part[direction, item, core]
            j = item // blocks
            e = direction * 2 * each + 2 * j + core
            high, low = split(side)
            add = dot(jnp.concatenate([high, high, low], axis=0), jnp.concatenate([high, low, high], axis=0), (0, 0))

            @pl.when(item % blocks == 0)
            def _():
                gram[j] = add

            @pl.when(item % blocks != 0)
            def _():
                gram[j] = gram[j] + add

            @pl.when(item % blocks == blocks - 1)
            def _():
                for r in range(n_tensor - 1, 0, -1):
                    enc_copy(j, e, r).start()
                enc[e] = gram[j, enc_rows(me), :]

    def step(s, carry):
        @pl.when(s < items)
        def _():
            slot = s % SLOTS

            @pl.when(s + SLOTS - 1 < items)
            def _():
                start_load(s + SLOTS - 1)

            pltpu.make_async_copy(x.at[slot], x.at[slot], x_sem.at[slot]).wait()
            sides = dot(x[slot].reshape(4 * CHUNK, width), w[...], (1, 0))
            for u in range(2):
                direction, item = where_is(s, u)
                part[direction, item] = sides[2 * u * CHUNK:2 * (u + 1) * CHUNK].reshape(2, CHUNK, 2 * rank)

            @pl.when(s == 0)
            def _():
                pl.semaphore_wait(barrier, n_tensor + n_dp - 2)
                for r in range(1, n_dp):
                    query_copy(r).start()

            for u in range(2):
                direction, item = where_is(s, u)
                pair_copy(direction, item).start()

        @pl.when(s == items)
        def _():
            q_own.wait()
            for r in range(1, n_dp):
                query_copy(r).wait_recv()
            high, low = split(q_all[...].reshape(q_high.shape))
            q_high[...] = high
            q_low[...] = low

        opening = s == near_hops + BASE
        first = jnp.where(is_end, 2 * (s - BASE), jnp.where(opening, 0, s - near_hops))
        count = jnp.where(jnp.logical_or(is_end, opening), 2, jnp.where(s > near_hops + BASE, 1, 0))
        for u in range(2):
            item = first + u

            @pl.when(jnp.logical_and(u < count, jnp.logical_and(item >= 0, item < items)))
            def _():
                process(near, item, near_hops)

        item_far = s - far_lag

        @pl.when(jnp.logical_and(item_far >= 0, item_far < items))
        def _():
            process(1 - near, item_far, far_hops)

        return carry

    lax.fori_loop(0, items + max(line - 1 + EXTRA, items // 2 + BASE), step, 0)

    for e in range(examples):
        owner = (0 if e < examples // 2 else n_tensor - 2) + e % 2

        @pl.when(me != owner)
        def _():
            enc_copy(0, e, 1).wait_recv()

    per = rank // n_tensor
    lane = lax.broadcasted_iota(jnp.int32, (examples, 2 * rank), 1)
    shift = me * per % group // per
    columns = []
    for m in range(per // 2):
        picked = None
        for v in range(group // per):
            low = enc[:, v * per + 2 * m, :]
            high = enc[:, v * per + 2 * m + 1, :]
            both = jnp.where(lane < rank, low, pltpu.roll(high, rank, 1))
            picked = both if picked is None else jnp.where(shift == v, both, picked)
        columns.append(picked)
    high, low = split(jnp.concatenate(columns, axis=1))
    both = dot(jnp.concatenate([high, low], axis=0), q_high[...], (1, 1))
    score[me] = both[:examples] + both[examples:] + dot(high, q_low[...], (1, 1))

    def score_copy(r):
        return pltpu.make_async_remote_copy(
            src_ref=score.at[me], dst_ref=score.at[me],
            send_sem=score_send.at[r - 1], recv_sem=score_recv.at[r - 1],
            device_id={"tensor": (me + r) % n_tensor}, device_id_type=MESH)

    def score_arrival(r):
        frm = (me - r + n_tensor) % n_tensor
        return pltpu.make_async_remote_copy(
            src_ref=score.at[frm], dst_ref=score.at[frm],
            send_sem=score_send.at[r - 1], recv_sem=score_recv.at[r - 1],
            device_id={"tensor": (me + r) % n_tensor}, device_id_type=MESH)

    for r in range(1, n_tensor):
        score_copy(r).start()
    for r in range(1, n_tensor):
        score_arrival(r).wait_recv()
    result = score[0]
    for t in range(1, n_tensor):
        result = result + score[t]
    out[...] = result * (length ** (-0.5) / rank)

    for r in range(1, n_tensor):
        score_copy(r).wait_send()
    for r in range(1, n_dp):
        query_copy(r).wait_send()

    def drain(i, carry):
        for direction in range(2):
            pair_copy(direction, i).wait_send()
            hops = jnp.where(near == direction, near_hops, far_hops)

            @pl.when(hops < line - 1)
            def _():
                chain_copy(direction, i).wait_send()

        return carry

    lax.fori_loop(0, items, drain, 0)

    @pl.when(is_end)
    def _():
        for j in range(each):
            for r in range(1, n_tensor):
                enc_copy(j, 0, r).wait_send()


def per_device(acts, grads, proj_in, proj_out, queries):
    examples, length, width_in = acts.shape
    width_out = grads.shape[2]
    rank = proj_in.shape[1]
    n_dp, n_tensor = lax.axis_size("dp"), lax.axis_size("tensor")
    n_query = queries.shape[0] * n_dp
    items = examples // 4 * (length // CHUNK)
    width = width_in + width_out
    group = max(rank // n_tensor, 8)
    f32, bf16, dma = jnp.float32, jnp.bfloat16, pltpu.SemaphoreType.DMA
    in_hbm = pl.BlockSpec(memory_space=pltpu.HBM)
    tokens = examples * length
    return pl.pallas_call(
        functools.partial(kernel, n_dp, n_tensor),
        out_shape=jax.ShapeDtypeStruct((examples, n_query), f32),
        in_specs=[in_hbm] * 5,
        out_specs=pl.BlockSpec(memory_space=pltpu.VMEM),
        scratch_shapes=[
            pltpu.VMEM((SLOTS, 4, CHUNK, width), bf16), dma((SLOTS,)),
            pltpu.VMEM((2 * rank, width), bf16), pltpu.VMEM((width, 2 * rank), bf16), dma((2,)),
            pltpu.VMEM((2, items, 2, CHUNK, 2 * rank), f32),
            pltpu.VMEM((2, items, CHUNK, 2 * rank), f32), dma((2, items)), dma((2, items)),
            pltpu.VMEM((2, items, CHUNK, 2 * rank), f32), dma((2, items)), dma((2, items)),
            pltpu.VMEM((examples // 4, 2 * rank, 2 * rank), f32),
            pltpu.VMEM((examples, group, 2 * rank), f32),
            dma((examples // 4, n_tensor - 1)), dma((examples,)),
            pltpu.VMEM((n_dp,) + queries.shape, f32),
            pltpu.VMEM((n_query, queries.shape[1]), bf16), pltpu.VMEM((n_query, queries.shape[1]), bf16), dma(()), dma((n_dp - 1,)), dma((n_dp - 1,)),
            pltpu.VMEM((n_tensor, examples, n_query), f32), dma((n_tensor - 1,)), dma((n_tensor - 1,)),
        ],
        compiler_params=pltpu.CompilerParams(
            collective_id=0, has_side_effects=True, vmem_limit_bytes=63 * 1024 * 1024),
        cost_estimate=pl.CostEstimate(
            flops=2 * tokens * width * rank, bytes_accessed=2 * tokens * width, transcendentals=0),
    )(acts, grads, proj_in.T, proj_out.T, queries)


def solution(mesh):
    in_specs = (
        P("dp", None, "tensor"),
        P("dp", None, "tensor"),
        P("tensor", None),
        P("tensor", None),
        P("dp", "tensor"),
    )
    out_specs = P("dp", None)
    return jax.shard_map(
        per_device, mesh=mesh, in_specs=in_specs, out_specs=out_specs, check_vma=False
    )
```
